128 devices in a mesh: blk: 4 (over y_lo, core), dp: 32 (over z, x, y_hi).
Axes of the slice: x: 4, y: 4 (y_hi: 2, y_lo: 2; y = y_hi * 2 + y_lo), z: 4, core: 2. Of those that a mesh axis runs over, the one named last changes fastest.
Arguments:
- image_features: bfloat16 [16384, 1152], P(('blk', 'dp')), may hold values from -12 to 12
- text_features: bfloat16 [16384, 1152], P(('blk', 'dp')), may hold values from -12 to 12
- image_head: bfloat16 [1152, 1152], replicated, may hold values from -1 to 1
- text_head: bfloat16 [1152, 1152], replicated, may hold values from -1 to 1
- scale: float32 [1], replicated, may hold values from 16 to 64
- offset: float32 [1], replicated, may hold values from -10 to -5
Outputs:
- image_head_grad: float32 [1152, 1152], replicated
- text_head_grad: float32 [1152, 1152], replicated
The draws below stay inside these ranges and needn't reach their ends.
All inputs are finite; a program needn't handle non-finite values.
Results may differ from the reference program's by a relative error of at most 0.0055.
Values may be sent and summed in bfloat16 or wider, within the bound.
A program may use at most 128 MiB of HBM per device.

```python
import math
import jax
import jax.numpy as jnp
from jax import lax

D = 1152
ROWS_DEV = 128
PAIRS = 16384
N_BLK = 4
N_DP = 32


def shared_pairs(key):
    clusters = max(PAIRS // 128, 4)
    labels = jax.random.randint(jax.random.fold_in(key, 101), (PAIRS,), 0, clusters)
    loading = jax.random.uniform(jax.random.fold_in(key, 102), (PAIRS, 1), jnp.float32, 0.5, 1.5)
    centers = jax.random.uniform(jax.random.fold_in(key, 103), (clusters, D), jnp.float32, 0.0001, 0.9999)
    private = jax.random.uniform(jax.random.fold_in(key, 104), (PAIRS, D), jnp.float32, 0.0001, 0.9999)
    return (labels, loading, centers, private)


def shared_head(key):
    return jax.random.uniform(jax.random.fold_in(key, 201), (D, D), jnp.float32, 0.0001, 0.9999)


def gaussian(probs):
    clipped = jnp.clip(probs, 0.001, 0.999)
    return 0.5513 * jnp.log(clipped / (1.0 - clipped))


def compose(centers, private, jitter, labels, loading):
    return loading * jnp.take(centers, labels, axis=0) + 0.8 * private + 0.6 * jitter


def mix_head(common, own):
    return (common + 0.5 * own) * (1.0 / math.sqrt(1.25 * D))


def draw_image_features(key, part):
    labels, loading, centers, private = shared_pairs(key)
    key = jax.random.fold_in(key, 7)
    jitter = jax.random.uniform(key, (PAIRS, D), jnp.float32, 0.0001, 0.9999)
    return compose(gaussian(centers), gaussian(private), gaussian(jitter), labels, loading).astype(jnp.bfloat16)


def draw_text_features(key, part):
    labels, loading, centers, private = shared_pairs(key)
    key = jax.random.fold_in(key, 8)
    jitter = jax.random.uniform(key, (PAIRS, D), jnp.float32, 0.0001, 0.9999)
    return compose(gaussian(centers), gaussian(private), gaussian(jitter), labels, loading).astype(jnp.bfloat16)


def draw_image_head(key, part):
    common = shared_head(key)
    key = jax.random.fold_in(key, 9)
    own = jax.random.uniform(key, (D, D), jnp.float32, 0.0001, 0.9999)
    return mix_head(gaussian(common), gaussian(own)).astype(jnp.bfloat16)


def draw_text_head(key, part):
    common = shared_head(key)
    key = jax.random.fold_in(key, 10)
    own = jax.random.uniform(key, (D, D), jnp.float32, 0.0001, 0.9999)
    return mix_head(gaussian(common), gaussian(own)).astype(jnp.bfloat16)


def setup_inputs(seed: int = 0) -> dict:
    key_list = jax.random.split(jax.random.key(seed), 7)
    return {
        "image_features": draw_image_features(jax.random.fold_in(key_list[6], 71), 0),
        "text_features": draw_text_features(jax.random.fold_in(key_list[6], 71), 0),
        "image_head": draw_image_head(jax.random.fold_in(key_list[6], 71), 0),
        "text_head": draw_text_head(jax.random.fold_in(key_list[6], 71), 0),
        "scale": jnp.clip(jnp.exp(jax.random.uniform(key_list[4], (1,), jnp.float32, math.log(16.0), math.log(64.0))), 16.0, 64.0),
        "offset": jnp.clip(jax.random.uniform(key_list[5], (1,), jnp.float32, -10.0, -5.0), -10.0, -5.0),
    }


EPS = 1e-06

def unit_rows(features, head):
    proj = jnp.dot(features, head, preferred_element_type=jnp.float32)
    norm = jnp.sqrt(lax.optimization_barrier(jnp.sum(proj * proj, axis=-1, keepdims=True)) + EPS)
    return (proj / norm, norm)

def pullback(unit, norm, grad):
    return (grad - unit * lax.optimization_barrier(jnp.sum(unit * grad, axis=-1, keepdims=True))) / norm

def member_sum(coef, rows, temper):
    coef_parts = coef.reshape(N_DP, ROWS_DEV, coef.shape[1])
    row_parts = rows.reshape(N_DP, ROWS_DEV, rows.shape[1])

    def add(total, pair):
        coef_piece, row_piece = pair
        term = temper * jnp.dot(coef_piece.T, row_piece, preferred_element_type=jnp.float32)
        rounded = lax.optimization_barrier(term.astype(jnp.bfloat16))
        return (total + rounded.astype(jnp.float32), None)
    start = jnp.zeros((coef.shape[1], rows.shape[1]), jnp.float32)
    total, unused = lax.scan(add, start, (coef_parts, row_parts))
    return total

def reference(image_features, text_features, image_head, text_head, scale, offset):
    temper = scale[0]
    shift_bias = offset[0]
    image_unit, image_norm = unit_rows(image_features, image_head)
    text_unit, text_norm = unit_rows(text_features, text_head)
    image_emb = image_unit.astype(jnp.bfloat16)
    text_emb = text_unit.astype(jnp.bfloat16)
    total = image_emb.shape[0]
    width = image_emb.shape[1]
    block = total // N_BLK
    local_ids = jnp.arange(block, dtype=jnp.int32)
    same_pair = (local_ids[:, None] == local_ids[None, :]).astype(jnp.float32)

    def step(text_dir, index):
        start = (index * block).astype(jnp.int32)
        prev_start = ((index + N_BLK - 1) % N_BLK * block).astype(jnp.int32)
        rows = lax.dynamic_slice_in_dim(image_emb, start, block, 0)
        own = lax.dynamic_slice_in_dim(text_emb, start, block, 0)
        prev = lax.dynamic_slice_in_dim(text_emb, prev_start, block, 0)
        logits_own = temper * jnp.einsum('id,jd->ij', rows.astype(jnp.float32), own.astype(jnp.float32)) + shift_bias
        logits_prev = temper * jnp.einsum('id,jd->ij', rows.astype(jnp.float32), prev.astype(jnp.float32)) + shift_bias
        coef_own = (jax.nn.sigmoid(logits_own) - same_pair).astype(jnp.bfloat16)
        coef_prev = jax.nn.sigmoid(logits_prev).astype(jnp.bfloat16)
        image_part = temper * jnp.dot(coef_own, own, preferred_element_type=jnp.float32) + temper * jnp.dot(coef_prev, prev, preferred_element_type=jnp.float32)
        own_add = member_sum(coef_own, rows, temper)
        prev_add = member_sum(coef_prev, rows, temper)
        zero = jnp.zeros((), jnp.int32)
        current = lax.dynamic_slice_in_dim(text_dir, start, block, 0)
        text_dir = lax.dynamic_update_slice(text_dir, current + own_add, (start, zero))
        current = lax.dynamic_slice_in_dim(text_dir, prev_start, block, 0)
        text_dir = lax.dynamic_update_slice(text_dir, current + prev_add, (prev_start, zero))
        return (text_dir, image_part)
    text_dir, image_parts = lax.scan(step, jnp.zeros((total, width), jnp.float32), jnp.arange(N_BLK, dtype=jnp.int32))
    image_dir = image_parts.reshape(total, width)
    image_back_low = pullback(image_unit, image_norm, image_dir).astype(jnp.bfloat16)
    text_back_low = pullback(text_unit, text_norm, text_dir).astype(jnp.bfloat16)
    image_grad = jnp.dot(image_features.T, image_back_low, preferred_element_type=jnp.float32)
    text_grad = jnp.dot(text_features.T, text_back_low, preferred_element_type=jnp.float32)
    return (image_grad, text_grad)
```

```python
import jax
import jax.numpy as jnp
from jax import lax
from jax.experimental import pallas as pl
from jax.experimental.pallas import tpu as pltpu
from jax.sharding import PartitionSpec as P

EPS = 1e-06
MESH = pl.DeviceIdType.MESH
D = 1152
ROWS = 128
UNIT = 256
UNITS = 5
TILE = 1024
HALF = 64
WIDE = D + 128
SPAN = 240.0


def position():
    blk, dp = lax.axis_index("blk"), lax.axis_index("dp")
    return {"z": dp // 8, "x": (dp // 2) % 4, "hi": dp % 2, "lo": blk // 2, "core": blk % 2}


def device(p):
    return (p["lo"] * 2 + p["core"], p["z"] * 8 + p["x"] * 2 + p["hi"])


def rings_of(p):
    y = p["hi"] * 2 + p["lo"]
    spots = [[(at + d) % 4 for d in range(4)] for at in (p["x"], y, p["z"])]
    places = [
        [{**p, "x": k} for k in spots[0]],
        [{**p, "hi": k // 2, "lo": k % 2} for k in spots[1]],
        [{**p, "z": k} for k in spots[2]],
    ]
    return spots, [[device(q) for q in ring] for ring in places]


def send(src, dst, send_sem, recv_sem, peer):
    return pltpu.make_async_remote_copy(
        src_ref=src, dst_ref=dst, send_sem=send_sem, recv_sem=recv_sem, device_id=peer, device_id_type=MESH
    )


def coded(total):
    top = jnp.max(jnp.abs(total), axis=-1, keepdims=True)
    scale = (jnp.maximum(top, 1e-30) * 1.01).astype(jnp.bfloat16)
    size = jnp.exp2(jnp.abs(total) * (SPAN / scale.astype(jnp.float32)) - SPAN / 2)
    return jnp.where(total < 0, -size, size).astype(jnp.bfloat16), scale


def decoded(rows):
    code = rows[:, :D].astype(jnp.float32)
    size = (jnp.log2(jnp.abs(code)) + SPAN / 2) * (rows[:, D : D + 1].astype(jnp.float32) / SPAN)
    return jnp.where(code < 0, -size, size)


def dot(a, b, over=((1,), (0,))):
    return lax.dot_general(a, b, (over, ((), ())), preferred_element_type=jnp.float32)


def kernel(
    scale, offset, img, txt, img_head, txt_head, out,
    fi, ft, ui, ut, ei, et, ni, nt, coef, back, part, pair, s1, r1, f2, s2, r2, r3, chunk,
    lsem, ts_s, ts_r, is_s, is_r, gi_s, gi_r, gt_s, gt_r,
    osem, p_s, p_r, a_s, a_r, b_s, b_r, c_s, c_r, d_s, d_r, e_s, e_r, m_s, m_r,
):
    p = position()
    x, z, hi, core = p["x"], p["z"], p["hi"], p["core"]
    blk = p["lo"] * 2 + core
    mate = device({**p, "core": 1 - core})
    twin = device({**p, "hi": 1 - hi})
    spots, peers = rings_of(p)

    def of_blk(b, h):
        return device({**p, "lo": b // 2, "core": b % 2, "hi": h})

    nxt = of_blk((blk + 1) % 4, 1)
    before = [of_blk((blk + 3) % 4, h) for h in (0, 1)]
    barrier = pltpu.get_barrier_semaphore()

    def greet(peer):
        pl.semaphore_signal(barrier, inc=1, device_id=peer, device_id_type=MESH)

    for ring in peers:
        for peer in ring[1:]:
            greet(peer)
    greet(mate)

    @pl.when(hi == 1)
    def _():
        greet(before[0])
        greet(before[1])

    wi, wt = part.at[pl.ds(0, D)], part.at[pl.ds(D, D)]
    load_wi = pltpu.make_async_copy(img_head, wi, lsem.at[0])
    load_wt = pltpu.make_async_copy(txt_head, wt, lsem.at[1])
    load_i = pltpu.make_async_copy(img, fi.at[pl.ds((hi * 4 + z) * ROWS, ROWS)], lsem.at[2])
    load_t = pltpu.make_async_copy(txt, ft.at[pl.ds(x * ROWS, ROWS)], lsem.at[3])
    load_i.start()
    load_wi.start()
    load_wt.start()

    @pl.when(hi == 0)
    def _():
        load_t.start()

    pl.semaphore_wait(barrier, 11)


    def piece(ref, h):
        return ref.at[pl.ds(h * HALF, HALF)]

    def rows(ref, s, at, h):
        return ref.at[pl.ds(pl.multiple_of((s * 4 + at) * ROWS + h * HALF, HALF), HALF)]

    def seed_t(k, h):
        return send(piece(txt, h), rows(ft, hi, x, h), ts_s.at[k, h], ts_r.at[hi, h], (nxt, twin)[k])

    def wait_seed_t(s, h):
        send(piece(txt, h), rows(ft, s, x, h), ts_s.at[0, h], ts_r.at[s, h], nxt).wait_recv()

    def seed_i(h):
        return send(piece(img, h), rows(fi, hi, z, h), is_s.at[h], is_r.at[h], twin)

    class Ring:
        def __init__(self, ref, axis, s_sem, r_sem):
            self.ref, self.s_sem, self.r_sem = ref, s_sem, r_sem
            self.spots, self.peers = spots[axis], peers[axis]

        def copy(self, s, kind, src=None):
            h = kind % 2
            at = self.spots[(0, 0, 3, 1)[kind // 2 + (kind == 5)]]
            peer = self.peers[(1, 3, 1, 3)[kind // 2 + (kind == 5)]]
            dst = rows(self.ref, s, at, h)
            return send(dst if src is None else piece(src, h), dst, self.s_sem.at[s, kind], self.r_sem.at[s, kind], peer)

        def start(self, s, h, src=None):
            self.copy(s, h, src).start()
            self.copy(s, 2 + h, src).start()

        def got(self, s, *kinds):
            for kind in kinds:
                self.copy(s, kind).wait_recv()

        def on(self, s):
            self.got(s, 0)
            self.copy(s, 4).start()
            self.got(s, 3)
            self.copy(s, 5).start()

        def sent(self):
            for s in (0, 1):
                for kind in range(6):
                    self.copy(s, kind).wait_send()

    ring_i = Ring(fi, 2, gi_s, gi_r)
    ring_t = Ring(ft, 0, gt_s, gt_r)

    for h in (0, 1):

        @pl.when(hi == 1)
        def _():
            seed_t(0, h).start()
            seed_t(1, h).start()

        @pl.when(hi == 0)
        def _():
            seed_t(0, h).start()
            ring_t.start(0, h, txt)

        ring_i.start(hi, h, img)

    def project(f, w, u, e, n, s, at, first, second):
        spots = [pl.ds(pl.multiple_of((s * 4 + at[k]) * ROWS, ROWS), ROWS) for k in (first, second)]
        proj = dot(jnp.concatenate([f[r] for r in spots], axis=0), w[...])
        inverse = 1.0 / jnp.sqrt(jnp.sum(proj * proj, axis=-1, keepdims=True) + EPS)
        unit = proj * inverse
        low = unit.astype(jnp.bfloat16)
        for k, r in enumerate(spots):
            half = slice(k * ROWS, (k + 1) * ROWS)
            u[r] = unit[half]
            e[r] = low[half]
            n[r] = inverse[half]

    def project_i(s, first, second):
        project(fi, wi, ui, ei, ni, s, spots[2], first, second)

    def project_t(s, first, second):
        project(ft, wt, ut, et, nt, s, spots[0], first, second)

    def texts_arrived(h):
        wait_seed_t(1, h)
        ring_t.start(1, h)

        @pl.when(hi == 1)
        def _():
            wait_seed_t(0, h)
            ring_t.start(0, h)

    texts_arrived(0)
    seed_i(0).start()
    seed_i(1).start()
    ring_i.on(hi)
    texts_arrived(1)
    load_i.wait()
    load_wi.wait()

    @pl.when(hi == 0)
    def _():
        load_t.wait()

    ring_i.got(hi, 1)
    project_i(hi, 0, 3)
    seed_i(0).wait_recv()
    ring_i.start(1 - hi, 0)
    ring_t.on(0)
    ring_i.got(hi, 2, 4, 5)
    project_i(hi, 1, 2)
    ring_t.on(1)
    seed_i(1).wait_recv()
    ring_i.start(1 - hi, 1)
    load_wt.wait()
    ring_t.got(0, 1)
    project_t(0, 0, 3)
    ring_t.got(0, 2, 4, 5)
    project_t(0, 1, 2)
    ring_i.on(1 - hi)
    ring_t.got(1, 1)
    project_t(1, 0, 3)
    ring_i.got(1 - hi, 1)
    project_i(1 - hi, 0, 3)
    ring_t.got(1, 2, 4, 5)
    project_t(1, 1, 2)
    ring_i.got(1 - hi, 2, 4, 5)
    project_i(1 - hi, 1, 2)


    temper = scale[0]
    shift_bias = offset[0]

    def sigmoid_of(a, b):
        logits = temper * dot(a, b, ((1,), (1,))) + shift_bias
        return 1.0 / (1.0 + jnp.exp(-logits))

    for k in range(4):
        r = slice(k * 256, (k + 1) * 256)
        coef[r] = sigmoid_of(ei[r], et[...]).astype(jnp.bfloat16)

    @pl.when(hi == 0)
    def _():
        ids = [lax.broadcasted_iota(jnp.int32, (ROWS, ROWS), k) for k in (0, 1)]
        same = jnp.where(ids[0] == ids[1], 1.0, 0.0)
        for s in (0, 1):
            r = pl.ds(pl.multiple_of((s * 4 + z) * ROWS, ROWS), ROWS)
            c = pl.ds(pl.multiple_of((s * 4 + x) * ROWS, ROWS), ROWS)
            coef[r, c] = (sigmoid_of(ei[r], et[c]) - same).astype(jnp.bfloat16)

    def pull(k, direction, u, n):
        r = slice(k * 256, (k + 1) * 256)
        unit = u[r]
        direction = temper * direction
        along_unit = jnp.sum(unit * direction, axis=-1, keepdims=True)
        back[r] = ((direction - unit * along_unit) * n[r]).astype(jnp.bfloat16)


    def swap(u):
        return send(part.at[pl.ds(u * UNIT, UNIT)], pair.at[u // 2], p_s.at[u // 2], p_r.at[u // 2], mate)

    def give(u):
        @pl.when(core != u % 2)
        def _():
            swap(u).start()

    def by_core(first, second):
        return first + core * (second - first)

    turn_spots = [[by_core(*v) for v in zip(spots[j], spots[(j + 1) % 3])] for j in range(3)]
    turn_peers = [
        [tuple(by_core(*v) for v in zip(*w)) for w in zip(peers[j], peers[(j + 1) % 3])] for j in range(3)
    ]
    core_row = core * UNIT

    def ring_of(l, k):
        return turn_spots[(2 * l + k) % 3], turn_peers[(2 * l + k) % 3]

    def stage1(l, d):
        at, peer = ring_of(l, 0)
        src = s1.at[l, pl.ds(pl.multiple_of(at[d] * 64, 64), 64)]
        return send(src, r1.at[l, d - 1], a_s.at[l, d - 1], a_r.at[l, d - 1], peer[d])

    def stage2(l, d):
        at, peer = ring_of(l, 1)
        src = s2.at[l, pl.ds(pl.multiple_of(at[d] * 16, 16), 16)]
        return send(src, r2.at[l, d - 1], b_s.at[l, d - 1], b_r.at[l, d - 1], peer[d])

    def stage3(l, d):
        at, peer = ring_of(l, 2)
        mine = r3.at[l, at[0]]
        return send(mine, mine, c_s.at[l, d - 1], c_r.at[l, d - 1], peer[d])

    def out_rows(l, first, count):
        return out.at[pl.ds(pl.multiple_of(l * 2 * UNIT + core_row + first, count), count)]

    rows16s = [out_rows(l, ring_of(l, 0)[0][0] * 64 + ring_of(l, 1)[0][0] * 16, 16) for l in range(UNITS)]

    def keep(l):
        return pltpu.make_async_copy(chunk.at[l], rows16s[l], osem.at[l])

    def inner(l, d):
        return send(chunk.at[l], rows16s[l], d_s.at[l, d - 1], d_r.at[l, d - 1], ring_of(l, 1)[1][d])

    def rows64(l, back):
        return out_rows(l, ring_of(l, 0)[0][(4 - back) % 4] * 64, 64)

    def outer(l, d):
        return send(rows64(l, 0), rows64(l, 0), e_s.at[l, d - 1], e_r.at[l, d - 1], ring_of(l, 0)[1][d])

    def over(l, back):
        return send(rows64(l, back), rows64(l, back), m_s.at[l, back], m_r.at[l, back], mate)

    def owned(step):
        def run(l):
            if l < UNITS - 1:
                step(l)
            else:
                pl.when(core == 0)(lambda: step(l))

        return run

    def part_rows(l, k):
        return pl.ds(pl.multiple_of(l * 2 * UNIT + core_row + k * 64, 64), 64)

    @owned
    def begin(l):
        swap(2 * l).wait_recv()

        def block(k, n):
            r = pl.ds(pl.multiple_of(k * 64, 64), 64)
            both = part[part_rows(l, k)].astype(jnp.float32) + pair[l, r].astype(jnp.float32)
            s1[l, r] = both.astype(jnp.bfloat16)
            return n

        lax.fori_loop(0, 4, block, 0)
        for d in (1, 3, 2):
            stage1(l, d).start()

    @owned
    def middle(l):
        for d in (1, 2, 3):
            stage1(l, d).wait_recv()
        k = ring_of(l, 0)[0][0]
        total = part[part_rows(l, k)].astype(jnp.float32)
        total = total + pair[l, pl.ds(pl.multiple_of(k * 64, 64), 64)].astype(jnp.float32)
        for d in range(3):
            total = total + r1[l, d].astype(jnp.float32)
        f2[l] = total
        s2[l] = total.astype(jnp.bfloat16)
        for d in (1, 3, 2):
            stage2(l, d).start()

    @owned
    def last(l):
        for d in (1, 2, 3):
            stage2(l, d).wait_recv()
        total = f2[l, pl.ds(pl.multiple_of(ring_of(l, 1)[0][0] * 16, 16), 16)]
        for d in range(3):
            total = total + r2[l, d].astype(jnp.float32)
        r3[l, ring_of(l, 2)[0][0]] = total
        for d in (1, 3, 2):
            stage3(l, d).start()

    @owned
    def finish(l):
        for d in (1, 2, 3):
            stage3(l, d).wait_recv()
        code, row_scale = coded(((r3[l, 0] + r3[l, 1]) + r3[l, 2]) + r3[l, 3])
        chunk[l, :, :D] = code
        chunk[l, :, D:] = jnp.broadcast_to(row_scale, (16, WIDE - D))
        keep(l).start()
        for d in (1, 3, 2):
            inner(l, d).start()

    @owned
    def around(l):
        keep(l).wait()
        for d in (1, 2, 3):
            inner(l, d).wait_recv()
        for d in (1, 3, 2):
            outer(l, d).start()
        over(l, 0).start()

    @owned
    def across(l):
        for d in (1, 3, 2):
            outer(l, d).wait_recv()
            over(l, d).start()

    @owned
    def drain(l):
        for d in (1, 2, 3):
            for stage in (stage1, stage2, stage3, inner, outer):
                stage(l, d).wait_send()
        for k in range(4):
            over(l, k).wait_send()

    def landed(l, back):
        r = out.at[pl.ds(pl.multiple_of(l * 2 * UNIT + UNIT - core_row + back * 64, 64), 64)]
        return send(r, r, m_s.at[l, back], m_r.at[l, back], mate)

    def arrive(l):
        def go():
            swap(2 * l).wait_send()
            for k in range(4):
                landed(l, k).wait_recv()

        if l < UNITS - 1:
            go()
        else:
            pl.when(core == 1)(go)

    def term(f, row, count, to):
        part[to : to + count] = dot(f[:, row : row + count], back[...], ((0,), (0,))).astype(jnp.bfloat16)

    for k in range(4):
        pull(k, dot(coef[k * 256 : (k + 1) * 256], et[...]), ui, ni)
    for u in range(4):
        term(fi, u * UNIT, UNIT, u * UNIT)
        give(u)
    term(fi, 1024, 128, 1024)

    def pull_text(k):
        pull(k, dot(coef[:, k * 256 : (k + 1) * 256], ei[...], ((0,), (0,))), ut, nt)

    pull_text(0)
    pull_text(1)
    begin(0)
    begin(1)
    pull_text(2)
    pull_text(3)
    term(ft, 0, 128, 1152)
    give(4)
    for u in range(5, 9):
        term(ft, u * UNIT - D, UNIT, u * UNIT)
        give(u)
        if u == 7:
            begin(2)
    begin(3)
    begin(4)
    for step in (middle, last, finish, around, across):
        for l in range(UNITS):
            step(l)


    for h in (0, 1):
        seed_t(0, h).wait_send()
        seed_i(h).wait_send()

        @pl.when(hi == 1)
        def _():
            seed_t(1, h).wait_send()

    ring_i.sent()
    ring_t.sent()
    for l in range(UNITS):
        drain(l)
        arrive(l)


def head_sums(scale, offset, img, txt, img_head, txt_head):
    dma = pltpu.SemaphoreType.DMA
    low, f32 = jnp.bfloat16, jnp.float32
    any_ = pl.BlockSpec(memory_space=pl.ANY)
    smem = pl.BlockSpec(memory_space=pltpu.SMEM)
    return pl.pallas_call(
        kernel,
        out_shape=jax.ShapeDtypeStruct((2 * D, WIDE), low),
        in_specs=[smem] * 2 + [any_] * 4,
        out_specs=any_,
        scratch_shapes=[pltpu.VMEM((TILE, D), low)] * 2
        + [pltpu.VMEM((TILE, D), f32)] * 2
        + [pltpu.VMEM((TILE, D), low)] * 2
        + [pltpu.VMEM((TILE, 1), f32)] * 2
        + [
            pltpu.VMEM((TILE, TILE), low),
            pltpu.VMEM((TILE, D), low),
            pltpu.VMEM((2 * D, D), low),
            pltpu.VMEM((UNITS, UNIT, D), low),
            pltpu.VMEM((UNITS, UNIT, D), low),
            pltpu.VMEM((UNITS, 3, 64, D), low),
            pltpu.VMEM((UNITS, 64, D), f32),
            pltpu.VMEM((UNITS, 64, D), low),
            pltpu.VMEM((UNITS, 3, 16, D), low),
            pltpu.VMEM((UNITS, 4, 16, D), f32),
            pltpu.VMEM((UNITS, 16, WIDE), low),
        ]
        + [dma((4,))]
        + [dma((2, 2))] * 2
        + [dma((2,))] * 2
        + [dma((2, 6))] * 4
        + [dma((UNITS,))] * 3
        + [dma((UNITS, 3))] * 10
        + [dma((UNITS, 4))] * 2,
        compiler_params=pltpu.CompilerParams(collective_id=0, has_side_effects=True, vmem_limit_bytes=62 << 20),
        name="head_sums",
    )(scale, offset, img, txt, img_head, txt_head)


def shards(image_features, text_features, image_head, text_head, scale, offset):
    rows = head_sums(scale, offset, image_features, text_features, image_head, text_head)
    return decoded(rows[:D]), decoded(rows[D:])


def solution(mesh):
    in_specs = (P(("blk", "dp"), None), P(("blk", "dp"), None), P(), P(), P(), P())
    out_specs = (P(), P())
    return jax.shard_map(shards, mesh=mesh, in_specs=in_specs, out_specs=out_specs, check_vma=False)
```
